256 devices in a mesh: blk: 64 (over x_hi, z, y), head: 4 (over x_lo, core).
Axes of the slice: x: 4 (x_hi: 2, x_lo: 2; x = x_hi * 2 + x_lo), y: 4, z: 8, core: 2. Of those that a mesh axis runs over, the one named last changes fastest.
Arguments:
- queries: bfloat16 [32768, 512], P('blk', 'head'), may hold values from -6 to 6
- keys: bfloat16 [32768, 512], P('blk', 'head'), may hold values from -6 to 6
- values: bfloat16 [32768, 512], P('blk', 'head'), may hold values from -6 to 6
- out_grad: bfloat16 [32768, 512], P('blk', 'head'), may hold values from -6 to 6
- w_out: bfloat16 [512, 512], P('head'), may hold values from -0.25 to 0.25
- slot_point: int32 [64, 1024], P('blk'), may hold values from 0 to 32767, as said below
- neighbours: int32 [64, 2], P('blk'), may hold values from 0 to 63, as said below
Outputs:
- query_grad: bfloat16 [32768, 512], P('blk', 'head')
- key_grad: bfloat16 [32768, 512], P('blk', 'head')
- value_grad: bfloat16 [32768, 512], P('blk', 'head')
- w_out_grad: float32 [512, 512], P('head')
The draws below stay inside these ranges and needn't reach their ends.
Inputs may be any that keep to these rules, and one draw needn't show every extreme that they name: `slot_point`: every entry of row p is one of the points p * 512 to p * 512 + 1023, taken modulo 32768; a point may fill several slots of a row, and some points of the range fill none. `neighbours`: row p holds 2 different patches p + o modulo 64, with o in -2 .. 2 and o not 0.
All inputs are finite; a program needn't handle non-finite values.
Results may differ from the reference program's by a relative error of at most 0.0065.
Values may be sent and summed in bfloat16 or wider, within the bound.
No kernel may reach another device: no remote copies, remote signals or barrier semaphores. Data moves between devices by JAX's collectives and lax.ppermute only.
A program may use at most 128 MiB of HBM per device.

```python
import jax
import jax.numpy as jnp
from jax import lax

D = 512
H = 8
HD = 64
S = 1024
HALF = 512
REACH = 2
NB = 2
NPATCH = 64
NPTS = 32768


def draw_queries(key, part):
    key = jax.random.fold_in(key, 5)
    base = jnp.clip(jax.random.normal(key, (NPTS, D)), -4.0, 4.0)
    return base.astype(jnp.bfloat16)


def draw_keys(key, part):
    key = jax.random.fold_in(key, 6)
    base = jnp.clip(jax.random.normal(key, (NPTS, D)), -4.0, 4.0)
    return base.astype(jnp.bfloat16)


def draw_slot_point(key, part):
    key = jax.random.fold_in(key, 7)
    perm_key, extra_key, pick_key = jax.random.split(key, 3)
    row_keys = jax.random.split(perm_key, NPATCH)
    perms = jax.vmap(lambda k: jax.random.permutation(k, S))(row_keys).astype(jnp.int32)
    extra = jax.random.randint(extra_key, (NPATCH, S), 0, S).astype(jnp.int32)
    picks = jax.random.randint(pick_key, (NPATCH, S), 0, 4) == 0
    local = jnp.where(picks, extra, perms)
    start = jnp.arange(NPATCH, dtype=jnp.int32)[:, None] * HALF
    return jnp.mod(start + local, NPTS).astype(jnp.int32)


def draw_neighbours(key, part):
    key = jax.random.fold_in(key, 8)
    offsets = jnp.concatenate([jnp.arange(-REACH, 0, dtype=jnp.int32), jnp.arange(1, REACH + 1, dtype=jnp.int32)])
    row_keys = jax.random.split(key, NPATCH)
    picks = jax.vmap(lambda k: jax.random.permutation(k, 2 * REACH)[:NB])(row_keys)
    chosen = offsets[picks]
    start = jnp.arange(NPATCH, dtype=jnp.int32)[:, None]
    return jnp.mod(start + chosen, NPATCH).astype(jnp.int32)


def levels(stream_key, dims, shards, smallest, high):
    def one(position, blocks):
        draws = jax.random.uniform(jax.random.fold_in(jax.random.fold_in(stream_key, 6), position), (blocks,), jnp.float32, smallest / len(shards), high / len(shards))
        return jnp.repeat(jnp.exp(draws), dims[position] // blocks).reshape((-1,) + (1,) * (len(dims) - position - 1))

    level = one(*shards[0])
    for cut in shards[1:]:
        level = level * one(*cut)
    return level


def noise(stream_key, extent, spread, limit, cuts=(), held_as=jnp.bfloat16):
    values = jax.random.normal(stream_key, extent, jnp.float32) * spread
    if len(cuts) > 0:
        values = levels(stream_key, extent, cuts, -0.22, 0.18) * values
    return jnp.clip(values, min=-limit, max=limit).astype(held_as)


def setup_inputs(seed: int = 0) -> dict:
    splits = jax.random.split(jax.random.key(seed), 8)
    queries = draw_queries(jax.random.fold_in(splits[7], 71), 0)
    keys = draw_keys(jax.random.fold_in(splits[7], 71), 0)
    values = noise(splits[2], (NPTS, D), 1.0, 6.0, ((0, 64), (1, 4)))
    out_grad = noise(splits[3], (NPTS, D), 1.0, 6.0, ((0, 64), (1, 4)))
    w_out = noise(splits[4], (D, D), D ** -0.5, 0.25, ((0, 4),))
    slot_point = draw_slot_point(jax.random.fold_in(splits[7], 71), 0)
    neighbours = draw_neighbours(jax.random.fold_in(splits[7], 71), 0)
    return dict(queries=queries, keys=keys, values=values, out_grad=out_grad, w_out=w_out, slot_point=slot_point, neighbours=neighbours)


def head_backward(q_h, k_h, v_h, d_h):
    scale = 1.0 / (q_h.shape[1] ** 0.5)
    scores = jnp.dot(q_h, k_h.T, preferred_element_type=jnp.float32) * scale
    peak = jnp.max(scores, axis=1, keepdims=True)
    weights = jnp.exp(scores - peak)
    probs = weights / jnp.sum(weights, axis=1, keepdims=True)
    probs_low = probs.astype(jnp.bfloat16)
    attn = jnp.dot(probs_low, v_h, preferred_element_type=jnp.float32).astype(jnp.bfloat16)
    d_probs = jnp.dot(d_h, v_h.T, preferred_element_type=jnp.float32)
    delta = jnp.sum(probs * d_probs, axis=1, keepdims=True)
    d_scores = (probs * (d_probs - delta) * scale).astype(jnp.bfloat16)
    d_query = jnp.dot(d_scores, k_h, preferred_element_type=jnp.float32)
    d_key = jnp.dot(d_scores.T, q_h, preferred_element_type=jnp.float32)
    d_value = jnp.dot(probs_low.T, d_h, preferred_element_type=jnp.float32)
    return attn, d_query, d_key, d_value


def reference(queries, keys, values, out_grad, w_out, slot_point, neighbours):
    npts = queries.shape[0]

    def patch_step(carry, patch):
        d_q, d_k, d_v, d_w = carry
        own = slot_point[patch]
        nbr = neighbours[patch]
        key_list = jnp.concatenate([own] + [slot_point[nbr[j]] for j in range(NB)])
        q_rows = queries[own]
        g_rows = out_grad[own]
        k_rows = keys[key_list]
        v_rows = values[key_list]
        d_attn = jnp.dot(g_rows, w_out.T, preferred_element_type=jnp.float32).astype(jnp.bfloat16)
        attn_all, dq_all, dk_all, dv_all = [], [], [], []
        for head_idx in range(H):
            cols = slice(head_idx * HD, (head_idx + 1) * HD)
            attn, dqh, dkh, dvh = head_backward(q_rows[:, cols], k_rows[:, cols], v_rows[:, cols], d_attn[:, cols])
            attn_all.append(attn)
            dq_all.append(dqh)
            dk_all.append(dkh)
            dv_all.append(dvh)
        attn_rows = jnp.concatenate(attn_all, axis=1)
        d_w = d_w + jnp.dot(attn_rows.T, g_rows, preferred_element_type=jnp.float32)
        d_q = d_q.at[own].add(jnp.concatenate(dq_all, axis=1))
        d_k = d_k.at[key_list].add(jnp.concatenate(dk_all, axis=1))
        d_v = d_v.at[key_list].add(jnp.concatenate(dv_all, axis=1))
        return (d_q, d_k, d_v, d_w), None

    zeros = jnp.zeros((npts, D), jnp.float32)
    start = (zeros, zeros, zeros, jnp.zeros((D, D), jnp.float32))
    final, _ = lax.scan(patch_step, start, jnp.arange(NPATCH, dtype=jnp.int32))
    d_q, d_k, d_v, d_w = final
    return d_q.astype(jnp.bfloat16), d_k.astype(jnp.bfloat16), d_v.astype(jnp.bfloat16), d_w
```

```python
import functools

import jax
import jax.numpy as jnp
from jax import lax
from jax.experimental import pallas as pl
from jax.experimental.pallas import tpu as pltpu
from jax.sharding import PartitionSpec as P

HD = 64
BLK = 512
WIN = 6 * BLK
TILE = 256
META = 32
UNIT = 2 * BLK + META
PLANES = 16
AXES = ("blk", "head")
F32 = jnp.float32
BF16 = jnp.bfloat16
ABSENT = -1e30


def device_id(plane, y, x, core):
    return ((plane % PLANES) * 4 + y % 4) * 4 + x * 2 + core


def send(block, target):
    route = []
    for plane in range(PLANES):
        for y in range(4):
            for x in range(2):
                for core in range(2):
                    there = target(plane, y, x, core)
                    if there is not None:
                        route.append((device_id(plane, y, x, core), device_id(*there)))
    return lax.ppermute(block, AXES, route)


def contract(a, b, dim_a, dim_b):
    return lax.dot_general(
        a, b, (((dim_a,), (dim_b,)), ((), ())), preferred_element_type=F32
    )


def attention_kernel(
    place_ref, plane_ref, left_ref, right_ref, last_ref,
    plane_out, edge_out, rows_out,
    kv, query, cot, meta, bias, weight, kv_acc, row_acc,
):
    core = place_ref[0]
    y = place_ref[1]

    def plane_rows(block, start, count):
        base = lax.rem(block - y + 4, 4) * UNIT + start
        return plane_ref[pl.ds(pl.multiple_of(base, META), count), :]

    lane = lax.broadcasted_iota(jnp.int32, (BLK, 2 * HD), 1)

    def put_query(slot, rows):
        zero = jnp.zeros_like(rows)
        at = pl.ds(slot * BLK, BLK)
        query[at, :] = jnp.where(lane < HD, rows * 0.125, zero)
        cot[at, :] = jnp.where(lane < HD, zero, rows)

    @pl.when(core == 0)
    def _():
        kv[0 : 2 * BLK, :] = left_ref[0 : 2 * BLK, :]
        kv[6 * BLK : 7 * BLK, :] = last_ref[...]
        meta[0 : 2 * META, :] = left_ref[2 * BLK : 2 * BLK + 2 * META, :]
        for block in range(4):
            kv[(2 + block) * BLK : (3 + block) * BLK, :] = plane_rows(block, 0, BLK)
            meta[(2 + block) * META : (3 + block) * META, :] = plane_rows(block, 2 * BLK, META)
        for slot in range(3):
            put_query(slot, plane_rows(slot, BLK, BLK))

    @pl.when(core == 1)
    def _():
        kv[4 * BLK : 7 * BLK, :] = right_ref[0 : 3 * BLK, :]
        meta[4 * META : 6 * META, :] = right_ref[4 * BLK : 4 * BLK + 2 * META, :]
        for block in range(4):
            kv[block * BLK : (1 + block) * BLK, :] = plane_rows(block, 0, BLK)
            meta[block * META : (1 + block) * META, :] = plane_rows(block, 2 * BLK, META)
        for slot in range(2):
            put_query(slot, plane_rows(2 + slot, BLK, BLK))
        put_query(2, right_ref[3 * BLK : 4 * BLK, :])

    def counts(patch):
        rows = meta[patch * META : (patch + 1) * META, :].astype(F32)
        return rows[0:8, :] * 32.0 + rows[8:16, :]

    eye = lax.broadcasted_iota(jnp.int32, (128, 128), 0) == lax.broadcasted_iota(
        jnp.int32, (128, 128), 1
    )
    for job in range(2):
        near = meta[(2 + job) * META + 16 : (2 + job) * META + 32, :].astype(F32)[0:1, :]

        def chosen(patch, near=near, job=job):
            if patch < 0 or patch > 5:
                return None
            if patch == 2 + job:
                return jnp.ones((1, 1), F32)
            offset = float(patch - 2 - job)
            hit = (near[:, 0:1] == offset) | (near[:, 1:2] == offset)
            return hit.astype(F32)

        for block in range(6):
            slot = block + job
            total = jnp.zeros((4, 128), F32)
            if abs(slot - 2 - job) <= 2 and slot <= 5:
                total = total + counts(slot)[0:4, :] * chosen(slot)
            if abs(slot - 3 - job) <= 2 and slot >= 1:
                total = total + counts(slot - 1)[4:8, :] * chosen(slot - 1)
            logs = jnp.where(total > 0.5, jnp.log(jnp.maximum(total, 1.0)), ABSENT)
            for row in range(4):
                at = block * BLK + row * 128
                bias[job, 0:1, at : at + 128] = logs[row : row + 1, :]
        own = counts(2 + job)
        for row in range(8):
            spread = jnp.where(eye, jnp.broadcast_to(own[row : row + 1, :], (128, 128)), 0.0)
            weight[job, row * 128 : (row + 1) * 128, :] = jnp.sum(spread, axis=1, keepdims=True)

    kv_acc[...] = jnp.zeros_like(kv_acc)
    row_acc[...] = jnp.zeros_like(row_acc)
    tile_lane = lax.broadcasted_iota(jnp.int32, (TILE, 2 * HD), 1)

    for job in range(2):

        def step(tile, carry, job=job):
            first = job * BLK
            keys = kv[first : first + WIN, :]
            rows = pl.ds(pl.multiple_of(first + tile * TILE, TILE), TILE)
            q = query[rows, :]
            d = cot[rows, :]
            times = weight[job, pl.ds(pl.multiple_of(tile * TILE, TILE), TILE), :]
            scores = contract(q, keys, 1, 1) + bias[job]
            peak = jnp.max(scores, axis=1, keepdims=True)
            grown = jnp.exp(scores - peak)
            probs = grown * (times / jnp.sum(grown, axis=1, keepdims=True))
            probs_low = probs.astype(BF16)
            attn = contract(probs_low, keys, 1, 0)
            d_probs = contract(d, keys, 1, 1)
            delta = jnp.sum(attn * d.astype(F32), axis=1, keepdims=True) / jnp.maximum(times, 1.0)
            d_scores = (probs * (d_probs - delta)).astype(BF16)
            d_query = contract(d_scores, keys, 1, 0) * 0.125
            row_acc[rows, :] += jnp.where(tile_lane < HD, d_query, attn)
            kv_acc[:, first : first + WIN] += contract(q, d_scores, 0, 0) + contract(
                d, probs_low, 0, 0
            )
            return carry

        lax.fori_loop(0, 2 * BLK // TILE, step, 0)

    rows_out[...] = row_acc[...].astype(BF16)

    def grads(slot):
        return kv_acc[:, slot * BLK : (slot + 1) * BLK].T.astype(BF16)

    edge_out[3 * BLK : 4 * BLK, :] = row_acc[2 * BLK : 3 * BLK, :].astype(BF16)

    @pl.when(core == 0)
    def _():
        for block in range(4):
            plane_out[block * BLK : (block + 1) * BLK, :] = grads(2 + block)
        for place, slot in enumerate((0, 1, 6)):
            edge_out[place * BLK : (place + 1) * BLK, :] = grads(slot)

    @pl.when(core == 1)
    def _():
        for block in range(4):
            plane_out[block * BLK : (block + 1) * BLK, :] = grads(block)
        for place, slot in enumerate((4, 5, 6)):
            edge_out[place * BLK : (place + 1) * BLK, :] = grads(slot)


def attention(place, plane, left, right, last):
    vmem = pl.BlockSpec(memory_space=pltpu.VMEM)
    return pl.pallas_call(
        attention_kernel,
        out_shape=(
            jax.ShapeDtypeStruct((4 * BLK, 2 * HD), BF16),
            jax.ShapeDtypeStruct((4 * BLK, 2 * HD), BF16),
            jax.ShapeDtypeStruct((3 * BLK, 2 * HD), BF16),
        ),
        in_specs=[pl.BlockSpec(memory_space=pltpu.SMEM)] + [vmem] * 4,
        out_specs=(vmem, vmem, vmem),
        scratch_shapes=[
            pltpu.VMEM((7 * BLK, 2 * HD), BF16),
            pltpu.VMEM((3 * BLK, 2 * HD), BF16),
            pltpu.VMEM((3 * BLK, 2 * HD), BF16),
            pltpu.VMEM((6 * META, 2 * HD), BF16),
            pltpu.VMEM((2, 1, WIN), F32),
            pltpu.VMEM((2, 2 * BLK, 1), F32),
            pltpu.VMEM((2 * HD, 7 * BLK), F32),
            pltpu.VMEM((3 * BLK, 2 * HD), F32),
        ],
        compiler_params=pltpu.CompilerParams(vmem_limit_bytes=56 * 1024 * 1024),
        cost_estimate=pl.CostEstimate(
            flops=40_000_000_000, bytes_accessed=4_000_000, transcendentals=6_300_000
        ),
        name="attention_backward",
    )(place, plane, left, right, last)


def local(queries, keys, values, out_grad, w_out, slot_point, neighbours):
    place = lax.axis_index("blk")
    head = lax.axis_index("head")
    y = lax.rem(place, 4)
    core = lax.rem(head, 2)
    anchor = y // 2
    npts = BLK * lax.axis_size("blk")
    blocks = lax.axis_size("blk")

    with jax.named_scope("cotangent"):
        grad_all = lax.all_gather(out_grad, "head", axis=1, tiled=True)
        d_attn = jnp.dot(grad_all, w_out.T, preferred_element_type=F32).astype(BF16)

    with jax.named_scope("units"):
        slots = jnp.mod(slot_point[0] - place * BLK, npts)
        bins = lax.broadcasted_iota(jnp.int32, (2 * BLK, 2 * BLK), 1)
        count = jnp.sum((slots[:, None] == bins).astype(jnp.int32), axis=0)
        offset = jnp.mod(neighbours[0] - place + blocks // 2, blocks) - blocks // 2
        near = jnp.pad(offset[None, :], ((0, 15), (0, 126)))
        meta = jnp.concatenate(
            [(count // 32).reshape(8, 128), (count % 32).reshape(8, 128), near]
        ).astype(BF16)

        def unit(j):
            cols = slice(j * HD, (j + 1) * HD)
            return jnp.concatenate(
                [
                    jnp.concatenate([keys[:, cols], values[:, cols]], axis=1),
                    jnp.concatenate([queries[:, cols], d_attn[:, cols]], axis=1),
                    meta,
                ]
            )

        units = (unit(0), unit(1))
        odd = lax.rem(y, 2) == 1
        same = jnp.where(odd, units[1], units[0])
        other = jnp.where(odd, units[0], units[1])

    def along_y(hops):
        def target(plane, y, x, core):
            there = (y + hops) % 4
            return (plane, there, x, core) if there // 2 == core else None

        return target

    with jax.named_scope("gather_y"):
        got = [send(same if k == 2 else other, along_y(k)) for k in (1, 2, 3)]
        held = jnp.concatenate([same, got[2], got[1], got[0]])

    with jax.named_scope("gather_z"):

        def held_unit(block):
            return lax.dynamic_slice_in_dim(held, lax.rem(block - y + 4, 4) * UNIT, UNIT, 0)

        first, second, third, fourth = [held_unit(i) for i in range(4)]
        kv_rows = slice(0, BLK)
        query_rows = slice(BLK, 2 * BLK)
        meta_rows = slice(2 * BLK, UNIT)
        from_left = jnp.concatenate(
            [third[kv_rows], fourth[kv_rows], third[meta_rows], fourth[meta_rows]]
        )
        from_right = jnp.concatenate(
            [
                first[kv_rows], second[kv_rows], third[kv_rows], first[query_rows],
                first[meta_rows], second[meta_rows],
            ]
        )
        shared = send(held, lambda p, y, x, c: (p, y, x, 1 - c) if c == y // 2 else None)
        left = send(from_left, lambda p, y, x, c: (p + 1, y, x, 0) if c == y // 2 else None)
        right = send(from_right, lambda p, y, x, c: (p - 1, y, x, 1) if c == y // 2 else None)
        last = send(first[kv_rows], lambda p, y, x, c: (p - 1, y, x, 0) if c == y // 2 else None)
        is_anchor = core == anchor
        plane = jnp.where(is_anchor, held, shared)

    with jax.named_scope("spread_grad"):
        grad_sent, plane, left, right, last = lax.optimization_barrier(
            (grad_all, plane, left, right, last)
        )

        def grad_target(hops):
            def target(p, y, x, c):
                if c == 0:
                    return (p, y + hops, x, c) if hops and y <= 2 else None
                if y == 0:
                    return (p - 1, hops, x, c)
                return (p, y + hops, x, c) if hops and y >= 2 else None

            return target

        grads = [send(grad_sent, grad_target(k)) for k in range(4)]

    with jax.named_scope("attention"):
        where = jnp.stack([core, y]).astype(jnp.int32)
        plane_grad, edge_grad, row_grad = attention(where, plane, left, right, last)

    with jax.named_scope("w_out_grad"):

        def attn_block(index):
            at = jnp.clip(index, 0, 2) * BLK
            return lax.dynamic_slice(row_grad, (at, HD), (BLK, HD))

        def part(index, grad):
            return lax.dot_general(
                attn_block(index), grad, (((0,), (0,)), ((), ())), preferred_element_type=F32
            )

        own_valid = jnp.where(core == 0, y <= 2, y >= 2)
        w_part = part(y - 2 * core, jnp.where(own_valid, grad_all, jnp.zeros_like(grad_all)))
        for k in range(4):
            index = jnp.where(
                core == 0,
                lax.rem(y - k + 4, 4),
                jnp.where(y == k, 2, lax.rem(y - k + 4, 4) - 2),
            )
            w_part = w_part + part(index, grads[k])
        w_low = w_part.astype(BF16)

    with jax.named_scope("return_z"):
        to_anchor = lambda p, y, x, c: (p, y, x, y // 2) if c != y // 2 else None
        w_pair = send(w_low, lambda p, y, x, c: (p, y, x, 1 - c))
        back_plane = send(plane_grad, to_anchor)
        back_rows = send(row_grad, to_anchor)
        back_right = send(
            edge_grad, lambda p, y, x, c: (p + 1, y, x, y // 2) if c == 1 else None
        )
        back_left = send(
            edge_grad[: 2 * BLK], lambda p, y, x, c: (p - 1, y, x, y // 2) if c == 0 else None
        )
        back_last = send(
            edge_grad[2 * BLK : 3 * BLK],
            lambda p, y, x, c: (p + 1, y, x, y // 2) if c == 0 else None,
        )

    with jax.named_scope("reduce_w"):
        w_sum = w_low.astype(F32) + w_pair.astype(F32)
        for stride in (1, 4):
            w_low = w_sum.astype(BF16)
            others = [
                send(w_low, lambda p, y, x, c, k=k: (p ^ (k * stride), y, x, c))
                for k in (1, 2, 3)
            ]
            w_sum = (w_low.astype(F32) + others[0].astype(F32)) + (
                others[1].astype(F32) + others[2].astype(F32)
            )
        w_low = w_sum.astype(BF16)

    with jax.named_scope("return_y"):
        plane_total = plane_grad.astype(F32) + back_plane.astype(F32)
        right_f = back_right.astype(F32)
        zero = jnp.zeros((BLK, 2 * HD), F32)
        plane_total = plane_total + jnp.concatenate(
            [right_f[:BLK] + back_last.astype(F32), right_f[BLK : 3 * BLK], zero]
        )
        plane_total = plane_total + jnp.concatenate([zero, zero, back_left.astype(F32)])
        low = jnp.where(core == 0, row_grad, back_rows).astype(F32)
        high = jnp.where(core == 0, back_rows, row_grad).astype(F32)
        rows_total = jnp.concatenate(
            [
                low[:BLK] + right_f[3 * BLK :],
                low[BLK : 2 * BLK],
                low[2 * BLK :] + high[:BLK],
                high[BLK : 2 * BLK],
            ]
        )
        result = jnp.concatenate(
            [
                plane_total.astype(BF16).reshape(4, BLK, 2 * HD),
                rows_total.astype(BF16).reshape(4, BLK, 2 * HD),
            ],
            axis=1,
        )

        def result_at(index):
            return lax.dynamic_index_in_dim(result, lax.rem(index, 4), 0, keepdims=False)

        def from_anchor(hops):
            return lambda p, y, x, c: (p, y + hops, x, c) if c == y // 2 else None

        parts = [result_at(y)] + [send(result_at(y + k), from_anchor(k)) for k in (1, 2, 3)]
        w_parts = [w_low] + [send(w_low, from_anchor(k)) for k in (1, 2, 3)]
        parts = jnp.stack(parts)
        w_parts = jnp.stack(w_parts)

        def head_part(stack, j):
            return lax.dynamic_index_in_dim(
                stack, lax.rem(y - 2 * core - j + 4, 4), 0, keepdims=False
            )

        heads = [head_part(parts, j) for j in range(2)]
        d_key = jnp.concatenate([u[:BLK, :HD] for u in heads], axis=1)
        d_value = jnp.concatenate([u[:BLK, HD:] for u in heads], axis=1)
        d_query = jnp.concatenate([u[BLK:, :HD] for u in heads], axis=1)
        w_grad = jnp.concatenate([head_part(w_parts, j) for j in range(2)]).astype(F32)
    return d_query, d_key, d_value, w_grad


def solution(mesh):
    placed = (
        P("blk", "head"),
        P("blk", "head"),
        P("blk", "head"),
        P("blk", "head"),
        P("head", None),
        P("blk", None),
        P("blk", None),
    )
    return jax.shard_map(
        local,
        mesh=mesh,
        in_specs=placed,
        out_specs=(P("blk", "head"), P("blk", "head"), P("blk", "head"), P("head", None)),
        check_vma=False,
    )
```

```python
import jax
import jax.numpy as jnp
from jax import lax
from jax.experimental import pallas as pl
from jax.experimental.pallas import tpu as pltpu
from jax.sharding import PartitionSpec as P

HD = 64
BLK = 512
HALF = BLK // 2
WIN = 6 * BLK
TILE = 256
META = 32
UNIT = BLK + META
FULL = UNIT + HALF
F32 = jnp.float32
BF16 = jnp.bfloat16
ABSENT = -1e30


def send(block, target):
    blocks = lax.axis_size("blk")
    route = [(i, target(i) % blocks) for i in range(blocks) if target(i) is not None]
    return lax.ppermute(block, "blk", route)


def swap(block, mask):
    return send(block, lambda i: i ^ mask)


def contract(a, b, dim_a, dim_b):
    return lax.dot_general(
        a, b, (((dim_a,), (dim_b,)), ((), ())), preferred_element_type=F32
    )


def lanes(rows):
    return lax.broadcasted_iota(jnp.int32, (rows, 2 * HD), 1)


def units_kernel(place_ref, near_ref, slots_ref, keys_ref, values_ref, queries_ref, own, theirs):
    place = place_ref[0]
    blocks = place_ref[1]
    slots = slots_ref[...] - place * BLK
    slots = jnp.where(slots < 0, slots + blocks * BLK, slots)
    high = lax.broadcasted_iota(jnp.int32, (16, 2 * BLK), 0)
    low = lax.broadcasted_iota(jnp.int32, (128, 2 * BLK), 0)
    row_hit = (high == lax.shift_right_logical(slots, 7)).astype(F32).astype(BF16)
    lane_hit = (low == (slots & 127)).astype(F32).astype(BF16)
    count = contract(row_hit, lane_hit, 1, 1)[0:8, :]
    coarse = jnp.floor(count * (1.0 / 32.0))

    def offset(j):
        hop = near_ref[0, j] - place
        hop = jnp.where(hop < -2, hop + blocks, hop)
        return jnp.where(hop > 2, hop - blocks, hop).astype(F32)

    lane = lanes(16)
    near = jnp.where(lane == 0, offset(0), jnp.where(lane == 1, offset(1), 0.0))
    meta = jnp.concatenate([coarse, count - coarse * 32.0, near]).astype(BF16)

    def rolled(rows):
        return pltpu.roll(rows.astype(F32), HD, 1).astype(BF16)

    keys = keys_ref[...]
    values = values_ref[...]
    top = queries_ref[0:HALF, :]
    end = queries_ref[HALF:BLK, :]
    left = lanes(BLK) < HD
    short = lanes(HALF) < HD

    def put(out, j):
        if j == 0:
            out[0:BLK, :] = jnp.where(left, keys, rolled(values))
            out[UNIT:FULL, :] = jnp.where(short, top, rolled(end))
        else:
            out[0:BLK, :] = jnp.where(left, rolled(keys), values)
            out[UNIT:FULL, :] = jnp.where(short, rolled(top), end)
        out[BLK:UNIT, :] = meta

    @pl.when(lax.rem(place, 2) == 0)
    def _():
        put(own, 0)
        put(theirs, 1)

    @pl.when(lax.rem(place, 2) == 1)
    def _():
        put(own, 1)
        put(theirs, 0)


def make_units(*operands):
    smem = pl.BlockSpec(memory_space=pltpu.SMEM)
    vmem = pl.BlockSpec(memory_space=pltpu.VMEM)
    unit = jax.ShapeDtypeStruct((FULL, 2 * HD), BF16)
    return pl.pallas_call(
        units_kernel,
        out_shape=(unit, unit),
        in_specs=[smem, smem] + [vmem] * 4,
        out_specs=(vmem, vmem),
        name="units",
    )(*operands)


def forward_prepare(
    member, own_ref, mate_ref, left_ref, right_ref, last_ref, kv, query, meta, bias, weight
):
    def put_keys(slot, rows):
        kv[pl.ds(pl.multiple_of(slot * BLK, BLK), BLK), :] = rows

    def put_meta(slot, rows):
        meta[pl.ds(pl.multiple_of(slot * META, META), META), :] = rows

    for near, far in ((own_ref, 0), (mate_ref, 1)):
        at = member if far == 0 else 1 - member
        put_keys(2 + at, near[0:BLK, :])
        put_meta(2 + at, near[BLK:UNIT, :])
        for first, pair in ((0, left_ref), (4, right_ref)):
            base = far * UNIT
            put_keys(first + at, pair[base : base + BLK, :])
            put_meta(first + at, pair[base + BLK : base + UNIT, :])
    put_keys(6, last_ref[...])

    def put_query(slot, rows):
        scaled = rows * 0.125
        zero = jnp.zeros_like(scaled)
        at = pl.multiple_of(slot * BLK, BLK)
        low = lanes(HALF) < HD
        flipped = pltpu.roll(scaled.astype(F32), HD, 1).astype(BF16)
        query[pl.ds(at, HALF), :] = jnp.where(low, scaled, zero)
        query[pl.ds(at + HALF, HALF), :] = jnp.where(low, flipped, zero)

    put_query(member, own_ref[UNIT:FULL, :])
    put_query(1 - member, mate_ref[UNIT:FULL, :])
    put_query(2, right_ref[2 * UNIT : 2 * UNIT + HALF, :])

    def counts(patch):
        rows = meta[patch * META : (patch + 1) * META, :].astype(F32)
        return rows[0:8, :] * 32.0 + rows[8:16, :]

    eye = lax.broadcasted_iota(jnp.int32, (128, 128), 0) == lax.broadcasted_iota(
        jnp.int32, (128, 128), 1
    )
    for job in range(2):
        near = meta[(2 + job) * META + 16 : (2 + job) * META + 32, :].astype(F32)[0:1, :]

        def chosen(patch, near=near, job=job):
            if patch < 0 or patch > 5:
                return None
            if patch == 2 + job:
                return jnp.ones((1, 1), F32)
            offset = float(patch - 2 - job)
            hit = (near[:, 0:1] == offset) | (near[:, 1:2] == offset)
            return hit.astype(F32)

        for block in range(6):
            slot = block + job
            total = jnp.zeros((4, 128), F32)
            if abs(slot - 2 - job) <= 2 and slot <= 5:
                total = total + counts(slot)[0:4, :] * chosen(slot)
            if abs(slot - 3 - job) <= 2 and slot >= 1:
                total = total + counts(slot - 1)[4:8, :] * chosen(slot - 1)
            logs = jnp.where(total > 0.5, jnp.log(jnp.maximum(total, 1.0)), ABSENT)
            for row in range(4):
                at = block * BLK + row * 128
                bias[job, 0:1, at : at + 128] = logs[row : row + 1, :]
        own = counts(2 + job)
        for row in range(8):
            spread = jnp.where(eye, jnp.broadcast_to(own[row : row + 1, :], (128, 128)), 0.0)
            weight[job, row * 128 : (row + 1) * 128, :] = jnp.sum(spread, axis=1, keepdims=True)


def attention_kernel(
    member_ref, own_ref, mate_ref, left_ref, right_ref, last_ref, cot_own, cot_mate, cot_rim,
    left_out, right_out, last_out, pair_out, mine_out, mate_out, rim_out,
    kv, query, cot, meta, bias, weight, kv_acc, row_acc,
):
    member = member_ref[0]
    forward_prepare(
        member, own_ref, mate_ref, left_ref, right_ref, last_ref, kv, query, meta, bias, weight
    )

    def put(slot, rows):
        zero = jnp.zeros_like(rows)
        at = pl.multiple_of(slot * BLK, BLK)
        high = lanes(HALF) >= HD
        flipped = pltpu.roll(rows.astype(F32), HD, 1).astype(BF16)
        cot[pl.ds(at, HALF), :] = jnp.where(high, flipped, zero)
        cot[pl.ds(at + HALF, HALF), :] = jnp.where(high, rows, zero)

    put(member, cot_own[...])
    put(1 - member, cot_mate[...])
    put(2, cot_rim[...])
    kv_acc[...] = jnp.zeros_like(kv_acc)
    row_acc[...] = jnp.zeros_like(row_acc)

    def step(tile, carry):
        keys = [kv[job * BLK : job * BLK + WIN, :] for job in range(2)]
        rows = [pl.ds(pl.multiple_of(job * BLK + tile * TILE, TILE), TILE) for job in range(2)]
        q = [query[at, :] for at in rows]
        d = [cot[at, :] for at in rows]
        at = pl.ds(pl.multiple_of(tile * TILE, TILE), TILE)
        times = [weight[job, at, :] for job in range(2)]

        def softmax(job):
            peak = jnp.max(scores[job], axis=1, keepdims=True)
            grown = jnp.exp(scores[job] - peak)
            probs = grown * (times[job] / jnp.sum(grown, axis=1, keepdims=True))
            return probs, probs.astype(BF16)

        def score_grads(job, probs, attn, d_probs):
            delta = jnp.sum(attn * d[job].astype(F32), axis=1, keepdims=True)
            delta = delta / jnp.maximum(times[job], 1.0)
            return (probs * (d_probs - delta)).astype(BF16)

        def gather_grads(job, low, attn, d_scores):
            d_query = contract(d_scores, keys[job], 1, 0) * 0.125
            row_acc[rows[job], :] += jnp.where(lanes(TILE) < HD, d_query, attn)
            first = job * BLK
            kv_acc[:, first : first + WIN] += contract(q[job], d_scores, 0, 0) + contract(
                d[job], low, 0, 0
            )

        scores = [contract(q[job], keys[job], 1, 1) + bias[job] for job in range(2)]
        probs_a, low_a = softmax(0)
        d_probs_a = contract(d[0], keys[0], 1, 1)
        attn_a = contract(low_a, keys[0], 1, 0)
        probs_b, low_b = softmax(1)
        d_scores_a = score_grads(0, probs_a, attn_a, d_probs_a)
        d_probs_b = contract(d[1], keys[1], 1, 1)
        attn_b = contract(low_b, keys[1], 1, 0)
        gather_grads(0, low_a, attn_a, d_scores_a)
        d_scores_b = score_grads(1, probs_b, attn_b, d_probs_b)
        gather_grads(1, low_b, attn_b, d_scores_b)
        return carry

    lax.fori_loop(0, 2 * BLK // TILE, step, 0)

    def grads(slot):
        return kv_acc[:, slot * BLK : (slot + 1) * BLK].T

    def packed_rows(slot):
        top = row_acc[slot * BLK : slot * BLK + HALF, :]
        low = row_acc[slot * BLK + HALF : (slot + 1) * BLK, :]
        return jnp.where(lanes(HALF) < HD, top, pltpu.roll(low, HD, 1))

    def packed_attn(slot):
        at = pl.multiple_of(slot * BLK, BLK)
        top = row_acc[pl.ds(at, HALF), :]
        low = row_acc[pl.ds(at + HALF, HALF), :]
        return jnp.where(lanes(HALF) < HD, pltpu.roll(top, HD, 1), low).astype(BF16)

    for block in range(2):
        at = slice(block * BLK, (block + 1) * BLK)
        left_out[at, :] = grads(block).astype(BF16)
        right_out[at, :] = grads(4 + block).astype(BF16)
        pair_out[block, 0:BLK, :] = grads(2 + block)
        pair_out[block, BLK : BLK + HALF, :] = packed_rows(block)
    right_out[2 * BLK : 2 * BLK + HALF, :] = packed_rows(2).astype(BF16)
    last_out[...] = grads(6).astype(BF16)
    mine_out[...] = packed_attn(member)
    mate_out[...] = packed_attn(1 - member)
    rim_out[...] = packed_attn(2)


def attention(*operands):
    vmem = pl.BlockSpec(memory_space=pltpu.VMEM)
    return pl.pallas_call(
        attention_kernel,
        out_shape=(
            jax.ShapeDtypeStruct((2 * BLK, 2 * HD), BF16),
            jax.ShapeDtypeStruct((2 * BLK + HALF, 2 * HD), BF16),
            jax.ShapeDtypeStruct((BLK, 2 * HD), BF16),
            jax.ShapeDtypeStruct((2, BLK + HALF, 2 * HD), F32),
            *[jax.ShapeDtypeStruct((HALF, 2 * HD), BF16)] * 3,
        ),
        in_specs=[pl.BlockSpec(memory_space=pltpu.SMEM)] + [vmem] * 8,
        out_specs=(vmem,) * 7,
        scratch_shapes=[
            pltpu.VMEM((7 * BLK, 2 * HD), BF16),
            pltpu.VMEM((3 * BLK, 2 * HD), BF16),
            pltpu.VMEM((3 * BLK, 2 * HD), BF16),
            pltpu.VMEM((6 * META, 2 * HD), BF16),
            pltpu.VMEM((2, 1, WIN), F32),
            pltpu.VMEM((2, 2 * BLK, 1), F32),
            pltpu.VMEM((2 * HD, 7 * BLK), F32),
            pltpu.VMEM((3 * BLK, 2 * HD), F32),
        ],
        compiler_params=pltpu.CompilerParams(vmem_limit_bytes=56 * 1024 * 1024),
        cost_estimate=pl.CostEstimate(
            flops=20_000_000_000, bytes_accessed=4_000_000, transcendentals=6_300_000
        ),
        name="attention_backward",
    )(*operands)


def local(queries, keys, values, out_grad, w_out, slot_point, neighbours):
    place = lax.axis_index("blk")
    blocks = lax.axis_size("blk")
    member = lax.rem(place, 2)
    second = member == 1
    flag = jnp.reshape(member, (1,)).astype(jnp.int32)

    def pick(if_first, if_second):
        return jnp.where(second, if_second, if_first)

    def folded(rows):
        return jnp.concatenate([rows[:HALF], rows[HALF:]], axis=1)

    def of_head(array, j):
        return array[:, j * HD : (j + 1) * HD]

    with jax.named_scope("units"):
        where = jnp.stack([place, jnp.full_like(place, blocks)]).astype(jnp.int32)
        own, theirs = make_units(where, neighbours, slot_point, keys, values, queries)

    with jax.named_scope("gather_keys"):
        mate = swap(theirs, 1)
        rim_query = pick(own[UNIT:], mate[UNIT:])
        pair = jnp.concatenate([own[:UNIT], mate[:UNIT], rim_query])
        left = send(pair[: 2 * UNIT], lambda i: i + 2)
        right = send(pair, lambda i: i - 2)
        last = send(pick(own[:BLK], mate[:BLK]), lambda i: i - 4)

    with jax.named_scope("cotangent"):
        head = lax.axis_index("head")
        got = [out_grad] + [
            lax.ppermute(out_grad, "head", [(i, i ^ k) for i in range(4)]) for k in (1, 2, 3)
        ]
        odd = lax.rem(head, 2) == 1
        got = [jnp.where(odd, got[k ^ 1], got[k]) for k in range(4)]
        upper = head >= 2
        grad_all = jnp.concatenate(
            [jnp.where(upper, got[k ^ 2], got[k]) for k in range(4)], axis=1
        )
        d_attn = jnp.dot(grad_all, w_out.T, preferred_element_type=F32).astype(BF16)
        cots = [folded(of_head(d_attn, j)) for j in range(2)]
        cot_own = pick(cots[0], cots[1])
        cot_mate = swap(pick(cots[1], cots[0]), 1)
        cot_rim = send(pick(cot_own, cot_mate), lambda i: i - 2)

    with jax.named_scope("attention"):
        left, right, last, cot_rim, grad_sent = lax.optimization_barrier(
            (left, right, last, cot_rim, grad_all)
        )
        grad_mate = swap(grad_sent, 1)
        left_grad, right_grad, last_grad, pair_grad, mine, theirs, rim = attention(
            flag, own, mate, left, right, last, cot_own, cot_mate, cot_rim
        )
        left_grad, right_grad, last_grad, pair_grad, mine, theirs, rim, grad_mate = (
            lax.optimization_barrier(
                (left_grad, right_grad, last_grad, pair_grad, mine, theirs, rim, grad_mate)
            )
        )

    half = blocks // 2
    planes = [
        [up * half + z * 4 + y for z in range(half // 4)] for up in range(2) for y in range(4)
    ]
    others = [
        [up * half + z * 4 + y for up in range(2) for y in range(4)] for z in range(half // 4)
    ]

    def exchange(rows, groups):
        return lax.all_to_all(rows, "blk", 0, 0, axis_index_groups=groups, tiled=True)

    def copies(rows):
        return jnp.broadcast_to(rows[None], (8,) + rows.shape).reshape(-1, rows.shape[1])

    with jax.named_scope("return_attention"):
        rim_got = send(rim, lambda i: i + 2)
        from_left = send(right_grad, lambda i: i + 2)
        from_right = send(left_grad, lambda i: i - 2)
        from_last = send(last_grad, lambda i: i + 4)

        def plus_rim(rows):
            return (rows.astype(F32) + rim_got.astype(F32)).astype(BF16)

        mine = pick(plus_rim(mine), mine)
        theirs = pick(theirs, plus_rim(theirs))

    with jax.named_scope("w_out_grad"):

        def part(attn, grad, half):
            return lax.dot_general(
                attn[:, half * HD : (half + 1) * HD],
                grad[half * HALF : (half + 1) * HALF],
                (((0,), (0,)), ((), ())),
                preferred_element_type=F32,
            )

        w_part = part(mine, grad_all, 0) + part(mine, grad_all, 1)
        w_part = w_part + part(theirs, grad_mate, 0) + part(theirs, grad_mate, 1)
        around = exchange(w_part, planes)
        around, from_left, from_right, from_last = lax.optimization_barrier(
            (around, from_left, from_right, from_last)
        )

    with jax.named_scope("totals"):
        from_left = from_left.astype(F32)
        from_right = from_right.astype(F32)
        first = pair_grad[0] + jnp.concatenate(
            [from_left[:BLK] + from_right[:BLK] + from_last.astype(F32), from_left[2 * BLK :]]
        )
        other = pair_grad[1] + jnp.concatenate(
            [from_left[BLK : 2 * BLK] + from_right[BLK:], jnp.zeros((HALF, 2 * HD), F32)]
        )
        mine = pick(first, other)
        got = swap(pick(other, first).astype(BF16), 1)
        width = around.shape[1]
        around = jnp.sum(around.reshape(8, HD // 8, width), axis=0)
        around = exchange(copies(around), others)
        around = jnp.sum(around.reshape(4, HD // 4, width), axis=0).astype(BF16)
        around, got = lax.optimization_barrier((around, got))
        around = exchange(copies(around), planes)
        around = jnp.swapaxes(around.reshape(8, 2, HD // 8, width), 0, 1)
        w_grad = around.reshape(2 * HD, width).astype(F32)
        heads = [pick(mine, got.astype(F32)), pick(got.astype(F32), mine)]
        d_key = jnp.concatenate([u[:BLK, :HD] for u in heads], axis=1).astype(BF16)
        d_value = jnp.concatenate([u[:BLK, HD:] for u in heads], axis=1).astype(BF16)
        d_query = jnp.concatenate(
            [jnp.concatenate([u[BLK:, :HD], u[BLK:, HD:]], axis=0) for u in heads], axis=1
        ).astype(BF16)
    return d_query, d_key, d_value, w_grad


def solution(mesh):
    placed = (
        P("blk", "head"),
        P("blk", "head"),
        P("blk", "head"),
        P("blk", "head"),
        P("head", None),
        P("blk", None),
        P("blk", None),
    )
    return jax.shard_map(
        local,
        mesh=mesh,
        in_specs=placed,
        out_specs=(P("blk", "head"), P("blk", "head"), P("blk", "head"), P("head", None)),
        check_vma=False,
    )
```

```python
import jax
import jax.numpy as jnp
from jax import lax
from jax.experimental import pallas as pl
from jax.experimental.pallas import tpu as pltpu
from jax.sharding import PartitionSpec as P

HD = 64
BLK = 512
HALF = BLK // 2
WIN = 6 * BLK
TILE = 256
META = 32
UNIT = BLK + META
F32 = jnp.float32
BF16 = jnp.bfloat16
ABSENT = -1e30


def send(block, target):
    blocks = lax.axis_size("blk")
    route = [(i, target(i) % blocks) for i in range(blocks) if target(i) is not None]
    return lax.ppermute(block, "blk", route)


def swap(block, mask):
    return send(block, lambda i: i ^ mask)


def contract(a, b, dim_a, dim_b):
    return lax.dot_general(
        a, b, (((dim_a,), (dim_b,)), ((), ())), preferred_element_type=F32
    )


def lanes(rows):
    return lax.broadcasted_iota(jnp.int32, (rows, 2 * HD), 1)


def units_kernel(
    near_ref, slots_ref, keys_ref, values_ref, queries_ref, own, theirs, own_rows, their_rows
):
    place = lax.axis_index("blk")
    blocks = lax.axis_size("blk")
    slots = slots_ref[...] - place * BLK
    slots = jnp.where(slots < 0, slots + blocks * BLK, slots)
    high = lax.broadcasted_iota(jnp.int32, (16, 2 * BLK), 0)
    low = lax.broadcasted_iota(jnp.int32, (128, 2 * BLK), 0)
    row_hit = (high == lax.shift_right_logical(slots, 7)).astype(F32).astype(BF16)
    lane_hit = (low == (slots & 127)).astype(F32).astype(BF16)
    count = contract(row_hit, lane_hit, 1, 1)[0:8, :]
    coarse = jnp.floor(count * (1.0 / 32.0))

    def offset(j):
        hop = near_ref[0, j] - place
        hop = jnp.where(hop < -2, hop + blocks, hop)
        return jnp.where(hop > 2, hop - blocks, hop).astype(F32)

    lane = lanes(16)
    near = jnp.where(lane == 0, offset(0), jnp.where(lane == 1, offset(1), 0.0))
    meta = jnp.concatenate([coarse, count - coarse * 32.0, near]).astype(BF16)

    def rolled(rows):
        return pltpu.roll(rows.astype(F32), HD, 1).astype(BF16)

    keys = keys_ref[...]
    values = values_ref[...]
    top = queries_ref[0:HALF, :]
    end = queries_ref[HALF:BLK, :]
    left = lanes(BLK) < HD
    short = lanes(HALF) < HD

    def put(out, rows_out, j):
        if j == 0:
            out[0:BLK, :] = jnp.where(left, keys, rolled(values))
            rows_out[...] = jnp.where(short, top, rolled(end))
        else:
            out[0:BLK, :] = jnp.where(left, rolled(keys), values)
            rows_out[...] = jnp.where(short, rolled(top), end)
        out[BLK:UNIT, :] = meta

    @pl.when(lax.rem(place, 2) == 0)
    def _():
        put(own, own_rows, 0)
        put(theirs, their_rows, 1)

    @pl.when(lax.rem(place, 2) == 1)
    def _():
        put(own, own_rows, 1)
        put(theirs, their_rows, 0)


def make_units(*operands):
    smem = pl.BlockSpec(memory_space=pltpu.SMEM)
    vmem = pl.BlockSpec(memory_space=pltpu.VMEM)
    unit = jax.ShapeDtypeStruct((UNIT, 2 * HD), BF16)
    rows = jax.ShapeDtypeStruct((HALF, 2 * HD), BF16)
    return pl.pallas_call(
        units_kernel,
        out_shape=(unit, unit, rows, rows),
        in_specs=[smem] + [vmem] * 4,
        out_specs=(vmem,) * 4,
        name="units",
    )(*operands)


def forward_prepare(
    place, own_ref, mate_ref, across_ref, beyond_ref, last_ref, kv, meta, bias, weight
):
    member = lax.rem(place, 2)
    upper = lax.rem(place, 4) // 2

    def put_keys(slot, rows):
        kv[pl.ds(pl.multiple_of(slot * BLK, BLK), BLK), :] = rows

    def put_meta(slot, rows):
        meta[pl.ds(pl.multiple_of(slot * META, META), META), :] = rows

    for near, far in ((own_ref, 0), (mate_ref, 1)):
        at = member if far == 0 else 1 - member
        put_keys(2 + at, near[0:BLK, :])
        put_meta(2 + at, near[BLK:UNIT, :])
        for first, pair in ((4 - 4 * upper, across_ref), (4 * upper, beyond_ref)):
            base = far * UNIT
            put_keys(first + at, pair[base : base + BLK, :])
            put_meta(first + at, pair[base + BLK : base + UNIT, :])
    put_keys(6, last_ref[...])

    def counts(patch):
        rows = meta[patch * META : (patch + 1) * META, :].astype(F32)
        return rows[0:8, :] * 32.0 + rows[8:16, :]

    eye = lax.broadcasted_iota(jnp.int32, (128, 128), 0) == lax.broadcasted_iota(
        jnp.int32, (128, 128), 1
    )
    for job in range(2):
        near = meta[(2 + job) * META + 16 : (2 + job) * META + 32, :].astype(F32)[0:1, :]

        def chosen(patch, near=near, job=job):
            if patch < 0 or patch > 5:
                return None
            if patch == 2 + job:
                return jnp.ones((1, 1), F32)
            offset = float(patch - 2 - job)
            hit = (near[:, 0:1] == offset) | (near[:, 1:2] == offset)
            return hit.astype(F32)

        for block in range(6):
            slot = block + job
            total = jnp.zeros((4, 128), F32)
            if abs(slot - 2 - job) <= 2 and slot <= 5:
                total = total + counts(slot)[0:4, :] * chosen(slot)
            if abs(slot - 3 - job) <= 2 and slot >= 1:
                total = total + counts(slot - 1)[4:8, :] * chosen(slot - 1)
            logs = jnp.where(total > 0.5, jnp.log(jnp.maximum(total, 1.0)), ABSENT)
            for row in range(4):
                at = block * BLK + row * 128
                bias[job, 0:1, at : at + 128] = logs[row : row + 1, :]
        own = counts(2 + job)
        for row in range(8):
            spread = jnp.where(eye, jnp.broadcast_to(own[row : row + 1, :], (128, 128)), 0.0)
            weight[job, row * 128 : (row + 1) * 128, :] = jnp.sum(spread, axis=1, keepdims=True)


def attention_kernel(
    own_ref, mate_ref, across_ref, beyond_ref, last_ref,
    own_rows, mate_rows, rim_rows,
    left_out, right_out, last_out, pair_out, mine_out, mate_out, rim_out,
    kv, query, cot, meta, bias, weight, kv_acc, row_acc,
):
    place = lax.axis_index("blk")
    member = lax.rem(place, 2)
    forward_prepare(
        place, own_ref, mate_ref, across_ref, beyond_ref, last_ref, kv, meta, bias, weight
    )

    def put(slot, rows):
        at = pl.multiple_of(slot * BLK, BLK)
        high = lanes(HALF) >= HD

        def unfold(out, part, start, keep):
            zero = jnp.zeros_like(part)
            other = pltpu.roll(part.astype(F32), HD, 1).astype(BF16)
            first, second = (other, part) if start else (part, other)
            out[pl.ds(at, HALF), :] = jnp.where(keep, first, zero)
            out[pl.ds(at + HALF, HALF), :] = jnp.where(keep, second, zero)

        unfold(query, rows[0:HALF, :] * 0.125, 0, ~high)
        unfold(cot, rows[HALF:BLK, :], 1, high)

    put(member, own_rows)
    put(1 - member, mate_rows)
    put(2, rim_rows)
    kv_acc[...] = jnp.zeros_like(kv_acc)
    row_acc[...] = jnp.zeros_like(row_acc)

    def step(tile, carry):
        keys = [kv[job * BLK : job * BLK + WIN, :] for job in range(2)]
        rows = [pl.ds(pl.multiple_of(job * BLK + tile * TILE, TILE), TILE) for job in range(2)]
        q = [query[at, :] for at in rows]
        d = [cot[at, :] for at in rows]
        at = pl.ds(pl.multiple_of(tile * TILE, TILE), TILE)
        times = [weight[job, at, :] for job in range(2)]

        def softmax(job):
            peak = jnp.max(scores[job], axis=1, keepdims=True)
            grown = jnp.exp(scores[job] - peak)
            share = times[job] / jnp.sum(grown, axis=1, keepdims=True)
            return share, grown.astype(BF16)

        def score_grads(job, share, low, attn, d_probs):
            delta = jnp.sum(attn * d[job].astype(F32), axis=1, keepdims=True)
            delta = delta / jnp.maximum(times[job], 1.0)
            return (low.astype(F32) * ((d_probs - delta) * share)).astype(BF16)

        def gather_grads(job, share, low, attn, d_scores):
            shared = (d[job].astype(F32) * share).astype(BF16)
            d_query = contract(d_scores, keys[job], 1, 0) * 0.125
            row_acc[rows[job], :] += jnp.where(lanes(TILE) < HD, d_query, attn)
            first = job * BLK
            kv_acc[:, first : first + WIN] += contract(q[job], d_scores, 0, 0) + contract(
                shared, low, 0, 0
            )

        scores = [contract(q[job], keys[job], 1, 1) + bias[job] for job in range(2)]
        share_a, low_a = softmax(0)
        d_probs_a = contract(d[0], keys[0], 1, 1)
        attn_a = contract(low_a, keys[0], 1, 0) * share_a
        share_b, low_b = softmax(1)
        d_scores_a = score_grads(0, share_a, low_a, attn_a, d_probs_a)
        d_probs_b = contract(d[1], keys[1], 1, 1)
        attn_b = contract(low_b, keys[1], 1, 0) * share_b
        gather_grads(0, share_a, low_a, attn_a, d_scores_a)
        d_scores_b = score_grads(1, share_b, low_b, attn_b, d_probs_b)
        gather_grads(1, share_b, low_b, attn_b, d_scores_b)
        return carry

    lax.fori_loop(0, 2 * BLK // TILE, step, 0)

    def grads(slot):
        return kv_acc[:, slot * BLK : (slot + 1) * BLK].T

    def packed_rows(slot):
        top = row_acc[slot * BLK : slot * BLK + HALF, :]
        low = row_acc[slot * BLK + HALF : (slot + 1) * BLK, :]
        return jnp.where(lanes(HALF) < HD, top, pltpu.roll(low, HD, 1))

    def packed_attn(slot):
        at = pl.multiple_of(slot * BLK, BLK)
        top = row_acc[pl.ds(at, HALF), :]
        low = row_acc[pl.ds(at + HALF, HALF), :]
        return jnp.where(lanes(HALF) < HD, pltpu.roll(top, HD, 1), low).astype(BF16)

    for block in range(2):
        at = slice(block * BLK, (block + 1) * BLK)
        left_out[at, :] = grads(block).astype(BF16)
        right_out[at, :] = grads(4 + block).astype(BF16)
        pair_out[block, 0:BLK, :] = grads(2 + block)
        pair_out[block, BLK : BLK + HALF, :] = packed_rows(block)
    right_out[2 * BLK : 2 * BLK + HALF, :] = packed_rows(2).astype(BF16)
    last_out[...] = grads(6).astype(BF16)
    mine_out[...] = packed_attn(member)
    mate_out[...] = packed_attn(1 - member)
    rim_out[...] = packed_attn(2)


def attention(*operands):
    vmem = pl.BlockSpec(memory_space=pltpu.VMEM)
    return pl.pallas_call(
        attention_kernel,
        out_shape=(
            jax.ShapeDtypeStruct((2 * BLK, 2 * HD), BF16),
            jax.ShapeDtypeStruct((2 * BLK + HALF, 2 * HD), BF16),
            jax.ShapeDtypeStruct((BLK, 2 * HD), BF16),
            jax.ShapeDtypeStruct((2, BLK + HALF, 2 * HD), F32),
            *[jax.ShapeDtypeStruct((HALF, 2 * HD), BF16)] * 3,
        ),
        in_specs=[vmem] * 8,
        out_specs=(vmem,) * 7,
        scratch_shapes=[
            pltpu.VMEM((7 * BLK, 2 * HD), BF16),
            pltpu.VMEM((3 * BLK, 2 * HD), BF16),
            pltpu.VMEM((3 * BLK, 2 * HD), BF16),
            pltpu.VMEM((6 * META, 2 * HD), BF16),
            pltpu.VMEM((2, 1, WIN), F32),
            pltpu.VMEM((2, 2 * BLK, 1), F32),
            pltpu.VMEM((2 * HD, 7 * BLK), F32),
            pltpu.VMEM((3 * BLK, 2 * HD), F32),
        ],
        compiler_params=pltpu.CompilerParams(vmem_limit_bytes=56 * 1024 * 1024),
        cost_estimate=pl.CostEstimate(
            flops=20_000_000_000, bytes_accessed=4_000_000, transcendentals=6_300_000
        ),
        name="attention_backward",
    )(*operands)


def local(queries, keys, values, out_grad, w_out, slot_point, neighbours):
    place = lax.axis_index("blk")
    blocks = lax.axis_size("blk")
    member = lax.rem(place, 2)
    second = member == 1

    def pick(if_first, if_second):
        return jnp.where(second, if_second, if_first)

    def folded(rows):
        return jnp.concatenate([rows[:HALF], rows[HALF:]], axis=1)

    def of_head(array, j):
        return array[:, j * HD : (j + 1) * HD]

    with jax.named_scope("units"):
        own, theirs, own_rows, their_rows = make_units(
            neighbours, slot_point, keys, values, queries
        )

    with jax.named_scope("gather_keys"):
        mate = swap(theirs, 1)
        pair = jnp.concatenate([own, mate])
        across = swap(pair, 2)
        beyond = send(across, lambda i: i + 4 if i % 4 < 2 else i - 4)
        last = send(pick(own[:BLK], mate[:BLK]), lambda i: i - 4)

    with jax.named_scope("cotangent"):
        head = lax.axis_index("head")
        got = [out_grad] + [
            lax.ppermute(out_grad, "head", [(i, i ^ k) for i in range(4)]) for k in (1, 2, 3)
        ]
        odd = lax.rem(head, 2) == 1
        got = [jnp.where(odd, got[k ^ 1], got[k]) for k in range(4)]
        upper = head >= 2
        grad_all = jnp.concatenate(
            [jnp.where(upper, got[k ^ 2], got[k]) for k in range(4)], axis=1
        )
        d_attn = jnp.dot(grad_all, w_out.T, preferred_element_type=F32).astype(BF16)
        cots = [folded(of_head(d_attn, j)) for j in range(2)]
        rows_own = jnp.concatenate([own_rows, pick(cots[0], cots[1])])
        rows_mate = swap(jnp.concatenate([their_rows, pick(cots[1], cots[0])]), 1)
        rows_rim = send(pick(rows_own, rows_mate), lambda i: i - 2)

    with jax.named_scope("attention"):
        across, beyond, last, rows_rim, grad_sent = lax.optimization_barrier(
            (across, beyond, last, rows_rim, grad_all)
        )
        grad_mate = swap(grad_sent, 1)
        left_grad, right_grad, last_grad, pair_grad, mine, theirs, rim = attention(
            own, mate, across, beyond, last, rows_own, rows_mate, rows_rim
        )
        left_grad, right_grad, last_grad, pair_grad, mine, theirs, rim, grad_mate = (
            lax.optimization_barrier(
                (left_grad, right_grad, last_grad, pair_grad, mine, theirs, rim, grad_mate)
            )
        )

    half = blocks // 2
    planes = [
        [up * half + z * 4 + y for z in range(half // 4)] for up in range(2) for y in range(4)
    ]
    others = [
        [up * half + z * 4 + y for up in range(2) for y in range(4)] for z in range(half // 4)
    ]

    def exchange(rows, groups):
        return lax.all_to_all(rows, "blk", 0, 0, axis_index_groups=groups, tiled=True)

    def copies(rows):
        return jnp.broadcast_to(rows[None], (8,) + rows.shape).reshape(-1, rows.shape[1])

    with jax.named_scope("return_attention"):
        rim_got = send(rim, lambda i: i + 2)
        from_left = send(right_grad, lambda i: i + 2)
        from_right = send(left_grad, lambda i: i - 2)
        from_last = send(last_grad, lambda i: i + 4)

        def plus_rim(rows):
            return (rows.astype(F32) + rim_got.astype(F32)).astype(BF16)

        mine = pick(plus_rim(mine), mine)
        theirs = pick(theirs, plus_rim(theirs))

    with jax.named_scope("w_out_grad"):

        def part(attn, grad, half):
            return lax.dot_general(
                attn[:, half * HD : (half + 1) * HD],
                grad[half * HALF : (half + 1) * HALF],
                (((0,), (0,)), ((), ())),
                preferred_element_type=F32,
            )

        w_part = part(mine, grad_all, 0) + part(mine, grad_all, 1)
        w_part = w_part + part(theirs, grad_mate, 0) + part(theirs, grad_mate, 1)
        around = exchange(w_part, planes)
        width = around.shape[1]
        around = jnp.sum(around.reshape(8, HD // 8, width), axis=0)
        around = exchange(copies(around), others)
        around = jnp.sum(around.reshape(4, HD // 4, width), axis=0).astype(BF16)

    with jax.named_scope("totals"):
        from_left = from_left.astype(F32)
        from_right = from_right.astype(F32)
        first = pair_grad[0] + jnp.concatenate(
            [from_left[:BLK] + from_right[:BLK] + from_last.astype(F32), from_left[2 * BLK :]]
        )
        other = pair_grad[1] + jnp.concatenate(
            [from_left[BLK : 2 * BLK] + from_right[BLK:], jnp.zeros((HALF, 2 * HD), F32)]
        )
        mine = pick(first, other)
        to_mate = pick(other, first).astype(BF16)
        around, to_mate = lax.optimization_barrier((copies(around), to_mate))
        got = swap(to_mate, 1)
        around = exchange(around, planes)
        around = jnp.swapaxes(around.reshape(8, 2, HD // 8, width), 0, 1)
        w_grad = around.reshape(2 * HD, width).astype(F32)
        heads = [pick(mine, got.astype(F32)), pick(got.astype(F32), mine)]
        d_key = jnp.concatenate([u[:BLK, :HD] for u in heads], axis=1).astype(BF16)
        d_value = jnp.concatenate([u[:BLK, HD:] for u in heads], axis=1).astype(BF16)
        d_query = jnp.concatenate(
            [jnp.concatenate([u[BLK:, :HD], u[BLK:, HD:]], axis=0) for u in heads], axis=1
        ).astype(BF16)
    return d_query, d_key, d_value, w_grad


def solution(mesh):
    placed = (
        P("blk", "head"),
        P("blk", "head"),
        P("blk", "head"),
        P("blk", "head"),
        P("head", None),
        P("blk", None),
        P("blk", None),
    )
    return jax.shard_map(
        local,
        mesh=mesh,
        in_specs=placed,
        out_specs=(P("blk", "head"), P("blk", "head"), P("blk", "head"), P("head", None)),
        check_vma=False,
    )
```

```python
import jax
import jax.numpy as jnp
from jax import lax
from jax.experimental import pallas as pl
from jax.experimental.pallas import tpu as pltpu
from jax.sharding import PartitionSpec as P

HD = 64
BLK = 512
HALF = BLK // 2
WIN = 6 * BLK
TILE = 512
META = 32
UNIT = BLK + META
F32 = jnp.float32
BF16 = jnp.bfloat16
ABSENT = -1e30


def send(block, target):
    blocks = lax.axis_size("blk")
    route = [(i, target(i) % blocks) for i in range(blocks) if target(i) is not None]
    return lax.ppermute(block, "blk", route)


def swap(block, mask):
    return send(block, lambda i: i ^ mask)


def contract(a, b, dim_a, dim_b):
    return lax.dot_general(
        a, b, (((dim_a,), (dim_b,)), ((), ())), preferred_element_type=F32
    )


def lanes(rows):
    return lax.broadcasted_iota(jnp.int32, (rows, 2 * HD), 1)


def units_kernel(
    near_ref, slots_ref, keys_ref, values_ref, queries_ref, own, theirs, own_rows, their_rows
):
    place = lax.axis_index("blk")
    blocks = lax.axis_size("blk")
    slots = slots_ref[...] - place * BLK
    slots = jnp.where(slots < 0, slots + blocks * BLK, slots)
    high = lax.broadcasted_iota(jnp.int32, (16, 2 * BLK), 0)
    low = lax.broadcasted_iota(jnp.int32, (128, 2 * BLK), 0)
    row_hit = (high == lax.shift_right_logical(slots, 7)).astype(F32).astype(BF16)
    lane_hit = (low == (slots & 127)).astype(F32).astype(BF16)
    count = contract(row_hit, lane_hit, 1, 1)[0:8, :]
    coarse = jnp.floor(count * (1.0 / 32.0))

    def offset(j):
        hop = near_ref[0, j] - place
        hop = jnp.where(hop < -2, hop + blocks, hop)
        return jnp.where(hop > 2, hop - blocks, hop).astype(F32)

    lane = lanes(16)
    near = jnp.where(lane == 0, offset(0), jnp.where(lane == 1, offset(1), 0.0))
    meta = jnp.concatenate([coarse, count - coarse * 32.0, near]).astype(BF16)

    def rolled(rows):
        return pltpu.roll(rows.astype(F32), HD, 1).astype(BF16)

    keys = keys_ref[...]
    values = values_ref[...]
    top = queries_ref[0:HALF, :]
    end = queries_ref[HALF:BLK, :]
    left = lanes(BLK) < HD
    short = lanes(HALF) < HD

    def put(out, rows_out, j):
        if j == 0:
            out[0:BLK, :] = jnp.where(left, keys, rolled(values))
            rows_out[...] = jnp.where(short, top, rolled(end))
        else:
            out[0:BLK, :] = jnp.where(left, rolled(keys), values)
            rows_out[...] = jnp.where(short, rolled(top), end)
        out[BLK:UNIT, :] = meta

    @pl.when(lax.rem(place, 2) == 0)
    def _():
        put(own, own_rows, 0)
        put(theirs, their_rows, 1)

    @pl.when(lax.rem(place, 2) == 1)
    def _():
        put(own, own_rows, 1)
        put(theirs, their_rows, 0)


def make_units(*operands):
    smem = pl.BlockSpec(memory_space=pltpu.SMEM)
    vmem = pl.BlockSpec(memory_space=pltpu.VMEM)
    unit = jax.ShapeDtypeStruct((UNIT, 2 * HD), BF16)
    rows = jax.ShapeDtypeStruct((HALF, 2 * HD), BF16)
    return pl.pallas_call(
        units_kernel,
        out_shape=(unit, unit, rows, rows),
        in_specs=[smem] + [vmem] * 4,
        out_specs=(vmem,) * 4,
        name="units",
    )(*operands)


def forward_prepare(
    place, own_ref, mate_ref, across_ref, beyond_ref, last_ref, kv, meta, bias, weight
):
    member = lax.rem(place, 2)
    upper = lax.rem(place, 4) // 2

    def put_keys(slot, rows):
        kv[pl.ds(pl.multiple_of(slot * BLK, BLK), BLK), :] = rows

    def put_meta(slot, rows):
        meta[pl.ds(pl.multiple_of(slot * META, META), META), :] = rows

    for near, far in ((own_ref, 0), (mate_ref, 1)):
        at = member if far == 0 else 1 - member
        put_keys(2 + at, near[0:BLK, :])
        put_meta(2 + at, near[BLK:UNIT, :])
        for first, pair in ((4 - 4 * upper, across_ref), (4 * upper, beyond_ref)):
            base = far * UNIT
            put_keys(first + at, pair[base : base + BLK, :])
            put_meta(first + at, pair[base + BLK : base + UNIT, :])
    put_keys(6, last_ref[...])

    def counts(patch):
        rows = meta[patch * META : (patch + 1) * META, :].astype(F32)
        return rows[0:8, :] * 32.0 + rows[8:16, :]

    eye = lax.broadcasted_iota(jnp.int32, (128, 128), 0) == lax.broadcasted_iota(
        jnp.int32, (128, 128), 1
    )
    for job in range(2):
        near = meta[(2 + job) * META + 16 : (2 + job) * META + 32, :].astype(F32)[0:1, :]

        def chosen(patch, near=near, job=job):
            if patch < 0 or patch > 5:
                return None
            if patch == 2 + job:
                return jnp.ones((1, 1), F32)
            offset = float(patch - 2 - job)
            hit = (near[:, 0:1] == offset) | (near[:, 1:2] == offset)
            return hit.astype(F32)

        for block in range(6):
            slot = block + job
            total = jnp.zeros((4, 128), F32)
            if abs(slot - 2 - job) <= 2 and slot <= 5:
                total = total + counts(slot)[0:4, :] * chosen(slot)
            if abs(slot - 3 - job) <= 2 and slot >= 1:
                total = total + counts(slot - 1)[4:8, :] * chosen(slot - 1)
            logs = jnp.where(total > 0.5, jnp.log(jnp.maximum(total, 1.0)), ABSENT)
            for row in range(4):
                at = block * BLK + row * 128
                bias[job, 0:1, at : at + 128] = logs[row : row + 1, :]
        own = counts(2 + job)
        for row in range(8):
            spread = jnp.where(eye, jnp.broadcast_to(own[row : row + 1, :], (128, 128)), 0.0)
            weight[job, row * 128 : (row + 1) * 128, :] = jnp.sum(spread, axis=1, keepdims=True)


def attention_kernel(
    own_ref, mate_ref, across_ref, beyond_ref, last_ref,
    own_rows, mate_rows, rim_rows,
    left_out, right_out, last_out, pair_out, mine_out, mate_out, rim_out,
    kv, query, cot, meta, bias, weight, kv_acc, row_acc,
):
    place = lax.axis_index("blk")
    member = lax.rem(place, 2)
    forward_prepare(
        place, own_ref, mate_ref, across_ref, beyond_ref, last_ref, kv, meta, bias, weight
    )

    def put(slot, rows):
        at = pl.multiple_of(slot * BLK, BLK)
        high = lanes(HALF) >= HD

        def unfold(out, part, start, keep):
            zero = jnp.zeros_like(part)
            other = pltpu.roll(part.astype(F32), HD, 1).astype(BF16)
            first, second = (other, part) if start else (part, other)
            out[pl.ds(at, HALF), :] = jnp.where(keep, first, zero)
            out[pl.ds(at + HALF, HALF), :] = jnp.where(keep, second, zero)

        unfold(query, rows[0:HALF, :] * 0.125, 0, ~high)
        unfold(cot, rows[HALF:BLK, :], 1, high)

    put(member, own_rows)
    put(1 - member, mate_rows)
    put(2, rim_rows)
    kv_acc[...] = jnp.zeros_like(kv_acc)
    row_acc[...] = jnp.zeros_like(row_acc)

    def step(tile, carry):
        keys = [kv[job * BLK : job * BLK + WIN, :] for job in range(2)]
        rows = [pl.ds(pl.multiple_of(job * BLK + tile * TILE, TILE), TILE) for job in range(2)]
        q = [query[at, :] for at in rows]
        d = [cot[at, :] for at in rows]
        at = pl.ds(pl.multiple_of(tile * TILE, TILE), TILE)
        times = [weight[job, at, :] for job in range(2)]

        def softmax(job):
            peak = jnp.max(scores[job], axis=1, keepdims=True)
            grown = jnp.exp(scores[job] - peak)
            share = times[job] / jnp.sum(grown, axis=1, keepdims=True)
            return share, grown.astype(BF16)

        def score_grads(job, share, low, attn, d_probs):
            delta = jnp.sum(attn * d[job].astype(F32), axis=1, keepdims=True)
            delta = delta / jnp.maximum(times[job], 1.0)
            return (low.astype(F32) * ((d_probs - delta) * share)).astype(BF16)

        def gather_grads(job, share, low, attn, d_scores):
            shared = (d[job].astype(F32) * share).astype(BF16)
            d_query = contract(d_scores, keys[job], 1, 0) * 0.125
            row_acc[rows[job], :] += jnp.where(lanes(TILE) < HD, d_query, attn)
            first = job * BLK
            kv_acc[:, first : first + WIN] += contract(q[job], d_scores, 0, 0) + contract(
                shared, low, 0, 0
            )

        scores = [contract(q[job], keys[job], 1, 1) + bias[job] for job in range(2)]
        share_a, low_a = softmax(0)
        d_probs_a = contract(d[0], keys[0], 1, 1)
        attn_a = contract(low_a, keys[0], 1, 0) * share_a
        share_b, low_b = softmax(1)
        d_scores_a = score_grads(0, share_a, low_a, attn_a, d_probs_a)
        d_probs_b = contract(d[1], keys[1], 1, 1)
        attn_b = contract(low_b, keys[1], 1, 0) * share_b
        gather_grads(0, share_a, low_a, attn_a, d_scores_a)
        d_scores_b = score_grads(1, share_b, low_b, attn_b, d_probs_b)
        gather_grads(1, share_b, low_b, attn_b, d_scores_b)
        return carry

    lax.fori_loop(0, 2 * BLK // TILE, step, 0)

    def grads(slot):
        return kv_acc[:, slot * BLK : (slot + 1) * BLK].T

    def packed_rows(slot):
        top = row_acc[slot * BLK : slot * BLK + HALF, :]
        low = row_acc[slot * BLK + HALF : (slot + 1) * BLK, :]
        return jnp.where(lanes(HALF) < HD, top, pltpu.roll(low, HD, 1))

    def packed_attn(slot):
        at = pl.multiple_of(slot * BLK, BLK)
        top = row_acc[pl.ds(at, HALF), :]
        low = row_acc[pl.ds(at + HALF, HALF), :]
        return jnp.where(lanes(HALF) < HD, pltpu.roll(top, HD, 1), low).astype(BF16)

    for block in range(2):
        at = slice(block * BLK, (block + 1) * BLK)
        left_out[at, :] = grads(block).astype(BF16)
        right_out[at, :] = grads(4 + block).astype(BF16)
        pair_out[block, 0:BLK, :] = grads(2 + block)
        pair_out[block, BLK : BLK + HALF, :] = packed_rows(block)
    right_out[2 * BLK : 2 * BLK + HALF, :] = packed_rows(2).astype(BF16)
    last_out[...] = grads(6).astype(BF16)
    mine_out[...] = packed_attn(member)
    mate_out[...] = packed_attn(1 - member)
    rim_out[...] = packed_attn(2)


def attention(*operands):
    vmem = pl.BlockSpec(memory_space=pltpu.VMEM)
    return pl.pallas_call(
        attention_kernel,
        out_shape=(
            jax.ShapeDtypeStruct((2 * BLK, 2 * HD), BF16),
            jax.ShapeDtypeStruct((2 * BLK + HALF, 2 * HD), BF16),
            jax.ShapeDtypeStruct((BLK, 2 * HD), BF16),
            jax.ShapeDtypeStruct((2, BLK + HALF, 2 * HD), F32),
            *[jax.ShapeDtypeStruct((HALF, 2 * HD), BF16)] * 3,
        ),
        in_specs=[vmem] * 8,
        out_specs=(vmem,) * 7,
        scratch_shapes=[
            pltpu.VMEM((7 * BLK, 2 * HD), BF16),
            pltpu.VMEM((3 * BLK, 2 * HD), BF16),
            pltpu.VMEM((3 * BLK, 2 * HD), BF16),
            pltpu.VMEM((6 * META, 2 * HD), BF16),
            pltpu.VMEM((2, 1, WIN), F32),
            pltpu.VMEM((2, 2 * BLK, 1), F32),
            pltpu.VMEM((2 * HD, 7 * BLK), F32),
            pltpu.VMEM((3 * BLK, 2 * HD), F32),
        ],
        compiler_params=pltpu.CompilerParams(vmem_limit_bytes=56 * 1024 * 1024),
        cost_estimate=pl.CostEstimate(
            flops=20_000_000_000, bytes_accessed=4_000_000, transcendentals=6_300_000
        ),
        name="attention_backward",
    )(*operands)


def local(queries, keys, values, out_grad, w_out, slot_point, neighbours):
    place = lax.axis_index("blk")
    blocks = lax.axis_size("blk")
    member = lax.rem(place, 2)
    second = member == 1

    def pick(if_first, if_second):
        return jnp.where(second, if_second, if_first)

    def folded(rows):
        return jnp.concatenate([rows[:HALF], rows[HALF:]], axis=1)

    def of_head(array, j):
        return array[:, j * HD : (j + 1) * HD]

    with jax.named_scope("units"):
        own, theirs, own_rows, their_rows = make_units(
            neighbours, slot_point, keys, values, queries
        )

    with jax.named_scope("gather_keys"):
        mate = swap(theirs, 1)
        pair = jnp.concatenate([own, mate])
        across = swap(pair, 2)
        beyond = send(across, lambda i: i + 4 if i % 4 < 2 else i - 4)
        last = send(pick(own[:BLK], mate[:BLK]), lambda i: i - 4)

    with jax.named_scope("cotangent"):
        head = lax.axis_index("head")
        got = [out_grad] + [
            lax.ppermute(out_grad, "head", [(i, i ^ k) for i in range(4)]) for k in (1, 2, 3)
        ]
        odd = lax.rem(head, 2) == 1
        got = [jnp.where(odd, got[k ^ 1], got[k]) for k in range(4)]
        upper = head >= 2
        grad_all = jnp.concatenate(
            [jnp.where(upper, got[k ^ 2], got[k]) for k in range(4)], axis=1
        )
        d_attn = jnp.dot(grad_all, w_out.T, preferred_element_type=F32).astype(BF16)
        cots = [folded(of_head(d_attn, j)) for j in range(2)]
        rows_own = jnp.concatenate([own_rows, pick(cots[0], cots[1])])
        rows_mate = swap(jnp.concatenate([their_rows, pick(cots[1], cots[0])]), 1)
        rows_rim = send(pick(rows_own, rows_mate), lambda i: i - 2)

    with jax.named_scope("attention"):
        across, beyond, last, rows_rim, grad_sent = lax.optimization_barrier(
            (across, beyond, last, rows_rim, grad_all)
        )
        grad_mate = swap(grad_sent, 1)
        left_grad, right_grad, last_grad, pair_grad, mine, theirs, rim = attention(
            own, mate, across, beyond, last, rows_own, rows_mate, rows_rim
        )
        left_grad, right_grad, last_grad, pair_grad, mine, theirs, rim, grad_mate = (
            lax.optimization_barrier(
                (left_grad, right_grad, last_grad, pair_grad, mine, theirs, rim, grad_mate)
            )
        )

    half = blocks // 2
    planes = [
        [up * half + z * 4 + y for z in range(half // 4)] for up in range(2) for y in range(4)
    ]
    others = [
        [up * half + z * 4 + y for up in range(2) for y in range(4)] for z in range(half // 4)
    ]

    def exchange(rows, groups):
        return lax.all_to_all(rows, "blk", 0, 0, axis_index_groups=groups, tiled=True)

    def copies(rows):
        return jnp.broadcast_to(rows[None], (8,) + rows.shape).reshape(-1, rows.shape[1])

    with jax.named_scope("return_attention"):
        rim_got = send(rim, lambda i: i + 2)
        from_left = send(right_grad, lambda i: i + 2)
        from_right = send(left_grad, lambda i: i - 2)
        from_last = send(last_grad, lambda i: i + 4)

        def plus_rim(rows):
            return (rows.astype(F32) + rim_got.astype(F32)).astype(BF16)

        mine = pick(plus_rim(mine), mine)
        theirs = pick(theirs, plus_rim(theirs))

    with jax.named_scope("w_out_grad"):

        def part(attn, grad, half):
            return lax.dot_general(
                attn[:, half * HD : (half + 1) * HD],
                grad[half * HALF : (half + 1) * HALF],
                (((0,), (0,)), ((), ())),
                preferred_element_type=F32,
            )

        w_part = part(mine, grad_all, 0) + part(mine, grad_all, 1)
        w_part = w_part + part(theirs, grad_mate, 0) + part(theirs, grad_mate, 1)
        around = exchange(w_part, planes)
        width = around.shape[1]
        around = jnp.sum(around.reshape(8, HD // 8, width), axis=0)
        around = exchange(copies(around), others)
        around = jnp.sum(around.reshape(4, HD // 4, width), axis=0).astype(BF16)

    with jax.named_scope("totals"):
        from_left = from_left.astype(F32)
        from_right = from_right.astype(F32)
        first = pair_grad[0] + jnp.concatenate(
            [from_left[:BLK] + from_right[:BLK] + from_last.astype(F32), from_left[2 * BLK :]]
        )
        other = pair_grad[1] + jnp.concatenate(
            [from_left[BLK : 2 * BLK] + from_right[BLK:], jnp.zeros((HALF, 2 * HD), F32)]
        )
        mine = pick(first, other)
        to_mate = pick(other, first).astype(BF16)
        around, to_mate = lax.optimization_barrier((copies(around), to_mate))
        got = swap(to_mate, 1)
        around = exchange(around, planes)
        around = jnp.swapaxes(around.reshape(8, 2, HD // 8, width), 0, 1)
        w_grad = around.reshape(2 * HD, width).astype(F32)
        heads = [pick(mine, got.astype(F32)), pick(got.astype(F32), mine)]
        d_key = jnp.concatenate([u[:BLK, :HD] for u in heads], axis=1).astype(BF16)
        d_value = jnp.concatenate([u[:BLK, HD:] for u in heads], axis=1).astype(BF16)
        d_query = jnp.concatenate(
            [jnp.concatenate([u[BLK:, :HD], u[BLK:, HD:]], axis=0) for u in heads], axis=1
        ).astype(BF16)
    return d_query, d_key, d_value, w_grad


def solution(mesh):
    placed = (
        P("blk", "head"),
        P("blk", "head"),
        P("blk", "head"),
        P("blk", "head"),
        P("head", None),
        P("blk", None),
        P("blk", None),
    )
    return jax.shard_map(
        local,
        mesh=mesh,
        in_specs=placed,
        out_specs=(P("blk", "head"), P("blk", "head"), P("blk", "head"), P("head", None)),
        check_vma=False,
    )
```
